32 devices in a mesh: dp: 2 (over y), expert: 16 (over z, x, core).
Axes of the slice: x: 2, y: 2, z: 4, core: 2. Of those that a mesh axis runs over, the one named last changes fastest.
Arguments:
- tokens: bfloat16 [2048, 4096], P('expert', 'dp'), may hold values from -6 to 6
- expert_ids: int32 [2048, 8], P('expert'), may hold values from 0 to 31, all different within a row; in each aligned block of 128 rows (0 to 127, 128 to 255, ...) at most 48 rows name the same one
- route_weights: float32 [2048, 8], P('expert'), may hold values from 0.1 to 0.4
- gate_up_weight: bfloat16 [32, 4096, 1536], P('expert', 'dp'), may hold values from -0.09375 to 0.09375
- down_weight: bfloat16 [32, 768, 4096], P('expert', None, 'dp'), may hold values from -0.21875 to 0.21875
- out_grad: bfloat16 [2048, 4096], P('expert', 'dp'), may hold values from -6 to 6
Outputs:
- layer_out: bfloat16 [2048, 4096], P('expert', 'dp')
- token_grad: bfloat16 [2048, 4096], P('expert', 'dp')
- route_grad: float32 [2048, 8], P('expert')
- gate_up_grad: bfloat16 [32, 4096, 1536], P('expert', 'dp')
- down_grad: bfloat16 [32, 768, 4096], P('expert', None, 'dp')
The draws below stay inside these ranges and needn't reach their ends.
Inputs may be any that keep to these rules, and one draw needn't show every extreme that they name: `expert_ids`: each row names 8 different experts. Among the 128 rows of one group no expert is named more than 48 times, and in every draw some group names some expert exactly 48 times.
All inputs are finite; a program needn't handle non-finite values.
Results may differ from the reference program's by a relative error of at most 0.029.
Values may be sent and summed in bfloat16 or wider, within the bound.
A program may use at most 128 MiB of HBM per device.

```python
import math
import jax
import jax.numpy as jnp
import numpy as np
from jax import lax

D = 4096
FF = 768
TOP = 8
TOK_DEV = 128
EXPERTS = 32
CAP = 48
TOKENS = 2048
N_DP = 2
N_EXPERT = 16


def levels(rng, extent, cuts, least, largest):
    loudness = 1.0
    for position, shards_of in cuts:
        draws = jax.random.uniform(jax.random.fold_in(jax.random.fold_in(rng, 6), position), (shards_of,), jnp.float32, least / len(cuts), largest / len(cuts))
        loudness = loudness * jnp.repeat(jnp.exp(draws), extent[position] // shards_of).reshape((-1,) + (1,) * (len(extent) - 1 - position))
    return loudness


def routed_block(stream_key, own, number, rows, amount, top, limit, lean):
    ranking = jax.random.permutation(stream_key, amount)
    crowded, usual = portions_of(amount, rows * top, limit, lean, True), portions_of(amount, rows * top, limit, lean, False)
    places = jnp.arange(amount)

    def named(tallies, rotation):
        used = int((tallies > 0).sum())
        fixed = max(1, used // 4)
        moved = fixed + (places - fixed + rotation * (used - fixed)) % max(1, amount - fixed)
        return jnp.zeros((amount,), jnp.int32).at[ranking[jnp.where(places < fixed, places, moved)]].set(jnp.asarray(tallies, jnp.int32))

    tallies = jnp.where(number % 4 == 0, named(crowded, number // 4), named(usual, number - number // 4 - 1))
    mixed = jax.random.permutation(jax.random.fold_in(own, 3), amount)
    source_of, receiver = mixed[0:amount // 2 * 2:2], mixed[1:amount // 2 * 2:2]
    margin = jnp.minimum(tallies[source_of] - 1, limit - tallies[receiver]) // 2
    margin = jnp.where((source_of == ranking[0]) | (receiver == ranking[0]) | (tallies[receiver] == 0), 0, jnp.maximum(margin, 0))
    moved = jax.random.randint(jax.random.fold_in(own, 4), (amount // 2,), 0, 1 << 20) % (margin + 1)
    tallies = tallies.at[source_of].add(-moved).at[receiver].add(moved)
    members = jnp.searchsorted(jnp.cumsum(tallies), jnp.arange(rows * top), side="right").astype(jnp.int32)
    grid = members.reshape(top, rows).T
    grid = grid[jax.random.permutation(jax.random.fold_in(own, 1), rows)]
    rotation = jax.random.randint(jax.random.fold_in(own, 2), (rows, 1), 0, top)
    return jnp.take_along_axis(grid, (jnp.arange(top)[None, :] + rotation) % top, axis=1)


def portions_of(amount, total, most, skew, full):
    portions = [(1 << 20) // math.isqrt(standing ** skew) + 1 for standing in range(1, amount + 1)]
    largest = most if full else min(most, max(-(-total // amount), total * portions[0] // sum(portions)))
    least = 1 if total - largest >= amount - 1 else 0
    counts, surplus = [largest] + [least] * (amount - 1), total - largest - least * (amount - 1)
    while surplus > 0:
        movable = [i for i in range(1, amount) if counts[i] < largest] or [i for i in range(1, amount) if counts[i] < most]
        pool, budget = sum([portions[i] for i in movable]), surplus
        for i in movable:
            addition = min(most - counts[i], max(1, budget * portions[i] // pool), surplus)
            counts[i] = counts[i] + addition
            surplus = surplus - addition
    return np.array(counts)


def gaussian(own_key, extent, deviation, reach, cuts=(), held_as=jnp.bfloat16):
    gain = levels(own_key, extent, cuts, -0.22, 0.18) if cuts else 1.0
    array = jax.random.normal(own_key, extent, jnp.float32) * deviation * gain
    return jnp.minimum(jnp.maximum(array, -reach), reach).astype(held_as)


def setup_inputs(seed: int = 0) -> dict:
    key_list = jax.random.split(jax.random.key(seed), 7)
    tokens = gaussian(key_list[0], (TOKENS, D), 1.0, 6.0, ((0, 16), (1, 2)))
    expert_ids_keys = jax.random.split(jax.random.fold_in(key_list[1], 1), TOKENS // TOK_DEV)
    expert_ids_turns = jax.random.permutation(jax.random.fold_in(key_list[1], 3), TOKENS // TOK_DEV)
    expert_ids = jax.vmap(lambda own, number: routed_block(jax.random.fold_in(key_list[1], 2), own, number, TOK_DEV, EXPERTS, TOP, CAP, 2))(expert_ids_keys, expert_ids_turns).reshape((TOKENS, TOP))
    route_weights = jnp.clip(0.1 + 0.3 * jax.random.uniform(key_list[2], (TOKENS, TOP), jnp.float32) ** levels(key_list[2], (TOKENS, TOP), ((0, 16),), -0.2, 0.2), 0.1, 0.4)
    gate_up_weight = gaussian(key_list[3], (EXPERTS, D, 2 * FF), D ** -0.5, 0.09375, ((0, 16), (1, 2)))
    down_weight = gaussian(key_list[4], (EXPERTS, FF, D), FF ** -0.5, 0.21875, ((0, 16), (2, 2)))
    out_grad = gaussian(key_list[5], (TOKENS, D), 1.0, 6.0, ((0, 16), (1, 2)))
    return dict(tokens=tokens, expert_ids=expert_ids, route_weights=route_weights, gate_up_weight=gate_up_weight, down_weight=down_weight, out_grad=out_grad)


def expert_pass(item):
    x_slots, dy_slots, w_gate_up, w_down = item
    row_total = x_slots.shape[0]
    piece_width = D // N_DP
    x_pieces = x_slots.reshape(row_total, N_DP, piece_width).astype(jnp.float32)
    w_pieces = w_gate_up.reshape(N_DP, piece_width, 2 * FF).astype(jnp.float32)
    partials = jnp.einsum('rjk,jkf->jrf', x_pieces, w_pieces)
    preact = jnp.sum(lax.optimization_barrier(partials.astype(jnp.bfloat16)).astype(jnp.float32), axis=0)
    gate_pre = preact[:, :FF]
    up_pre = preact[:, FF:]
    sigmoid_gate = jax.nn.sigmoid(gate_pre)
    activation = gate_pre * sigmoid_gate
    hidden = (activation * up_pre).astype(jnp.bfloat16)
    y_slots = jnp.dot(hidden, w_down, preferred_element_type=jnp.float32).astype(jnp.bfloat16)
    dy_pieces = dy_slots.reshape(row_total, N_DP, piece_width).astype(jnp.float32)
    wd_pieces = w_down.astype(jnp.float32).reshape(FF, N_DP, piece_width)
    grad_parts = jnp.einsum('rjk,fjk->jrf', dy_pieces, wd_pieces)
    hidden_grad = jnp.sum(lax.optimization_barrier(grad_parts.astype(jnp.bfloat16)).astype(jnp.float32), axis=0)
    gate_grad = hidden_grad * up_pre * sigmoid_gate * (1.0 + gate_pre * (1.0 - sigmoid_gate))
    up_grad = hidden_grad * activation
    preact_grad = jnp.concatenate([gate_grad, up_grad], axis=1).astype(jnp.bfloat16)
    x_grad = jnp.dot(preact_grad, w_gate_up.T, preferred_element_type=jnp.float32).astype(jnp.bfloat16)
    gate_up_grad = jnp.dot(x_slots.T, preact_grad, preferred_element_type=jnp.float32).astype(jnp.bfloat16)
    down_grad = jnp.dot(hidden.T, dy_slots, preferred_element_type=jnp.float32).astype(jnp.bfloat16)
    return y_slots, x_grad, gate_up_grad, down_grad


def reference(tokens, expert_ids, route_weights, gate_up_weight, down_weight, out_grad):
    group_total = N_EXPERT
    grouped = expert_ids.reshape(group_total, TOK_DEV * TOP)
    onehot = (grouped[:, :, None] == jnp.arange(EXPERTS, dtype=jnp.int32)[None, None, :]).astype(jnp.int32)
    slot_rank = jnp.sum(onehot * (jnp.cumsum(onehot, axis=1) - 1), axis=2)
    group_ids = jnp.arange(group_total, dtype=jnp.int32)[:, None]
    route_rows = (grouped * (group_total * CAP) + group_ids * CAP + slot_rank).reshape(-1).astype(jnp.int32)
    slot_total = EXPERTS * group_total * CAP
    token_routes = jnp.repeat(tokens, TOP, axis=0)
    x_all = jnp.zeros((slot_total, D), jnp.bfloat16).at[route_rows].set(token_routes)
    weight_flat = route_weights.reshape(-1)
    grad_routes = jnp.repeat(out_grad.astype(jnp.float32), TOP, axis=0)
    dy_all = jnp.zeros((slot_total, D), jnp.bfloat16).at[route_rows].set((weight_flat[:, None] * grad_routes).astype(jnp.bfloat16))
    y_all, dx_all, gate_up_grad, down_grad = lax.map(expert_pass, (x_all.reshape(EXPERTS, group_total * CAP, D), dy_all.reshape(EXPERTS, group_total * CAP, D), gate_up_weight, down_weight))
    y_routes = y_all.reshape(slot_total, D)[route_rows].astype(jnp.float32)
    layer_out = (weight_flat[:, None] * y_routes).reshape(TOKENS, TOP, D).sum(axis=1).astype(jnp.bfloat16)
    route_grad = jnp.sum(grad_routes * y_routes, axis=1).reshape(TOKENS, TOP)
    dx_routes = dx_all.reshape(slot_total, D)[route_rows].astype(jnp.float32)
    token_grad = dx_routes.reshape(TOKENS, TOP, D).sum(axis=1).astype(jnp.bfloat16)
    return layer_out, token_grad, route_grad, gate_up_grad, down_grad
```

```python
import jax
import jax.numpy as jnp
from jax import lax
from jax.sharding import PartitionSpec as P

BF16 = jnp.bfloat16
F32 = jnp.float32


def dot(a, b, contract):
    return lax.dot_general(a, b, (contract, ((), ())), preferred_element_type=F32)


def dp_sum(part):
    size = lax.axis_size("dp")
    if size == 2:
        other = lax.ppermute(part, "dp", [(0, 1), (1, 0)])
        return part.astype(F32) + other.astype(F32)
    return lax.psum(part.astype(F32), "dp")


def local(tokens, expert_ids, route_weights, gate_up_weight, down_weight, out_grad):
    tok_count, width = tokens.shape
    top_count = expert_ids.shape[1]
    groups = lax.axis_size("expert")
    local_count = gate_up_weight.shape[0]
    units = down_weight.shape[1]
    experts = local_count * groups
    capacity = 3 * tok_count * top_count // (2 * experts)
    rows = groups * capacity
    me = lax.axis_index("expert")

    routing = lax.all_gather(
        jnp.concatenate([expert_ids.astype(F32), route_weights], axis=1),
        "expert",
        axis=0,
        tiled=True,
    ).reshape(groups, tok_count, 2 * top_count)
    x_all = lax.all_gather(tokens, "expert", axis=0, tiled=True)
    og_all = lax.all_gather(out_grad, "expert", axis=0, tiled=True)
    x_all = x_all.reshape(groups, tok_count, width)
    og_all = og_all.reshape(groups, tok_count, width)

    ids = routing[..., :top_count]
    weights = routing[..., top_count:]
    mine = me * local_count + jnp.arange(local_count)
    hits = ids[None] == mine.astype(F32)[:, None, None, None]
    chosen = jnp.any(hits, axis=3)
    token_weight = jnp.sum(jnp.where(hits, weights[None], 0.0), axis=3)
    before = jnp.arange(tok_count)[:, None] < jnp.arange(tok_count)[None, :]
    rank = jnp.einsum(
        "lgt,tu->lgu", chosen.astype(BF16), before.astype(BF16), preferred_element_type=F32
    )
    places = jnp.arange(capacity, dtype=jnp.int32).astype(F32)
    picks = chosen[:, :, None, :] & (rank[:, :, None, :] == places[None, None, :, None])
    pick = picks.astype(BF16)
    slot_weight = jnp.sum(jnp.where(picks, token_weight[:, :, None, :], 0.0), axis=3)

    def slots(array, l):
        return (
            jnp.einsum("gct,gtd->gcd", pick[l], array, preferred_element_type=F32)
            .astype(BF16)
            .reshape(rows, width)
        )

    def combine(values):
        total = sum(
            jnp.einsum(
                "gct,gcd->gtd",
                pick[l],
                values[l].reshape(groups, capacity, width),
                preferred_element_type=F32,
            )
            for l in range(local_count)
        )
        return lax.psum_scatter(
            total.astype(BF16).reshape(groups * tok_count, width),
            "expert",
            scatter_dimension=0,
            tiled=True,
        )

    each = range(local_count)
    x_slots = [slots(x_all, l) for l in each]
    og_slots = [slots(og_all, l) for l in each]
    preact = [dp_sum(dot(x_slots[l], gate_up_weight[l], ((1,), (0,))).astype(BF16)) for l in each]
    raw_grad = [dp_sum(dot(og_slots[l], down_weight[l], ((1,), (1,))).astype(BF16)) for l in each]
    hidden_w, preact_grad, route_part = [], [], []
    for l in each:
        w = slot_weight[l].reshape(rows, 1)
        gate, up = preact[l][:, :units], preact[l][:, units:]
        sig = jax.nn.sigmoid(gate)
        act = gate * sig
        hidden = act * up
        hidden_w.append((w * hidden).astype(BF16))
        route_part.append(jnp.sum(hidden * raw_grad[l], axis=1).reshape(groups, capacity))
        grad = w * raw_grad[l]
        preact_grad.append(
            jnp.concatenate(
                [grad * up * sig * (1.0 + gate * (1.0 - sig)), grad * act], axis=1
            ).astype(BF16)
        )
    layer_out = combine([dot(hidden_w[l], down_weight[l], ((1,), (0,))).astype(BF16) for l in each])
    token_grad = combine(
        [dot(preact_grad[l], gate_up_weight[l], ((1,), (1,))).astype(BF16) for l in each]
    )
    gate_up_grad = jnp.stack(
        [dot(x_slots[l], preact_grad[l], ((0,), (0,))).astype(BF16) for l in each]
    )
    down_grad = jnp.stack([dot(hidden_w[l], og_slots[l], ((0,), (0,))).astype(BF16) for l in each])
    route_token = jnp.stack(
        [jnp.sum(jnp.where(picks[l], route_part[l][:, :, None], 0.0), axis=1) for l in each]
    )
    route_all = jnp.sum(jnp.where(hits, route_token[..., None], 0.0), axis=0)
    route_grad = lax.psum_scatter(
        route_all.reshape(groups * tok_count, top_count),
        "expert",
        scatter_dimension=0,
        tiled=True,
    )
    return layer_out, token_grad, route_grad, gate_up_grad, down_grad


def solution(mesh):
    placed = (
        P("expert", "dp"),
        P("expert", None),
        P("expert", None),
        P("expert", "dp", None),
        P("expert", None, "dp"),
        P("expert", "dp"),
    )
    return jax.shard_map(
        local,
        mesh=mesh,
        in_specs=placed,
        out_specs=(
            P("expert", "dp"),
            P("expert", "dp"),
            P("expert", None),
            P("expert", "dp", None),
            P("expert", None, "dp"),
        ),
        check_vma=False,
    )
```

```python
import jax
import jax.numpy as jnp
from jax import lax
from jax.sharding import PartitionSpec as P

BF16 = jnp.bfloat16
F32 = jnp.float32


def dot(a, b, contract):
    return lax.dot_general(a, b, (contract, ((), ())), preferred_element_type=F32)


def dp_sum(part):
    size = lax.axis_size("dp")
    if size == 2:
        other = lax.ppermute(part, "dp", [(0, 1), (1, 0)])
        return part.astype(F32) + other.astype(F32)
    return lax.psum(part.astype(F32), "dp")


def ring_step(axis_size, step):
    chips = axis_size // 2
    order = [2 * i if 2 * i < chips else 2 * (chips - 1 - i) + 1 for i in range(chips)]
    return [
        (2 * order[i] + core, 2 * order[(i + step) % chips] + core)
        for i in range(chips)
        for core in range(2)
    ]


def move(array, step):
    return lax.ppermute(array, "expert", ring_step(lax.axis_size("expert"), step))


def swap(array):
    size = lax.axis_size("expert")
    return lax.ppermute(array, "expert", [(i, i ^ 1) for i in range(size)])


def hops(more):
    chips = lax.axis_size("expert") // 2
    return (chips // 2, chips - 1 - chips // 2) if more else (chips - 1 - chips // 2, chips // 2)


def after(array, earlier):
    return lax.optimization_barrier((array, earlier))[0]


def gather_ring(shard, more, behind=None):
    chips = lax.axis_size("expert") // 2
    ahead, back = hops(more)
    held = [None] * chips
    held[0] = shard
    first = shard if behind is None else after(shard, behind[0])
    second = shard if behind is None else after(shard, behind[1])
    for hop in range(1, max(ahead, back) + 1):
        if hop <= ahead:
            first = move(first, 1)
            held[hop] = first
        if hop <= back:
            second = move(second, -1)
            held[chips - hop] = second
    return jnp.stack(held + [swap(piece) for piece in held]), (first, second)


def scatter_ring(parts, more):
    chips = parts.shape[0] // 2
    ahead, back = hops(more)
    paired = swap(parts[chips:])

    def mine(o):
        return parts[o].astype(F32) + paired[o].astype(F32)

    first, second = mine(chips - ahead), mine(back)
    for hop in range(max(ahead, back) - 1, -1, -1):
        if hop < ahead:
            first = move(first.astype(BF16), 1).astype(F32)
            if hop:
                first = first + mine(chips - hop)
        if hop < back:
            second = move(second.astype(BF16), -1).astype(F32)
            if hop:
                second = second + mine(hop)
    return (mine(0) + first + second).astype(BF16)


def reorder(array, index):
    pick = index[:, None] == jnp.arange(array.shape[0])[None, :]
    return jnp.sum(jnp.where(pick[:, :, None, None], array[None], 0.0), axis=1)


def local(tokens, expert_ids, route_weights, gate_up_weight, down_weight, out_grad):
    tok_count, width = tokens.shape
    top_count = expert_ids.shape[1]
    groups = lax.axis_size("expert")
    local_count = gate_up_weight.shape[0]
    units = down_weight.shape[1]
    experts = local_count * groups
    capacity = 3 * tok_count * top_count // (2 * experts)
    rows = groups * capacity
    me = lax.axis_index("expert")

    chips = groups // 2
    spot = jnp.arange(groups)
    place = jnp.where(spot // 2 % 2 == 0, spot // 4, chips - 1 - spot // 4)
    my_place = jnp.where(me // 2 % 2 == 0, me // 4, chips - 1 - me // 4)
    where = (my_place - place) % chips + jnp.where(spot % 2 == me % 2, 0, chips)
    chip_at = (my_place - spot % chips) % chips
    chip_at = jnp.where(2 * chip_at < chips, 2 * chip_at, 2 * (chips - 1 - chip_at) + 1)
    order = 2 * chip_at + (me % 2 + spot // chips) % 2

    x_all, ends = gather_ring(tokens, True)
    og_all, _ = gather_ring(out_grad, False, ends)
    routing = lax.all_gather(
        jnp.concatenate([expert_ids.astype(F32), route_weights], axis=1),
        "expert",
        axis=0,
        tiled=True,
    ).reshape(groups, tok_count, 2 * top_count)
    routing = reorder(routing, order)

    ids = routing[..., :top_count]
    weights = routing[..., top_count:]
    mine = me * local_count + jnp.arange(local_count)
    hits = ids[None] == mine.astype(F32)[:, None, None, None]
    chosen = jnp.any(hits, axis=3)
    token_weight = jnp.sum(jnp.where(hits, weights[None], 0.0), axis=3)
    before = jnp.arange(tok_count)[:, None] < jnp.arange(tok_count)[None, :]
    rank = jnp.einsum(
        "lgt,tu->lgu", chosen.astype(BF16), before.astype(BF16), preferred_element_type=F32
    )
    places = jnp.arange(capacity, dtype=jnp.int32).astype(F32)
    picks = chosen[:, :, None, :] & (rank[:, :, None, :] == places[None, None, :, None])
    pick = picks.astype(BF16)
    slot_weight = jnp.sum(jnp.where(picks, token_weight[:, :, None, :], 0.0), axis=3)

    def slots(array, l):
        return (
            jnp.einsum("gct,gtd->gcd", pick[l], array, preferred_element_type=F32)
            .astype(BF16)
            .reshape(rows, width)
        )

    def combine(values, more):
        total = sum(
            jnp.einsum(
                "gct,gcd->gtd",
                pick[l],
                values[l].reshape(groups, capacity, width),
                preferred_element_type=F32,
            )
            for l in range(local_count)
        )
        return scatter_ring(total.astype(BF16), more)

    each = range(local_count)
    x_slots = [slots(x_all, l) for l in each]
    og_slots = [slots(og_all, l) for l in each]
    preact = [dp_sum(dot(x_slots[l], gate_up_weight[l], ((1,), (0,))).astype(BF16)) for l in each]
    raw_grad = [dp_sum(dot(og_slots[l], down_weight[l], ((1,), (1,))).astype(BF16)) for l in each]
    hidden_w, preact_grad, route_part = [], [], []
    for l in each:
        w = slot_weight[l].reshape(rows, 1)
        gate, up = preact[l][:, :units], preact[l][:, units:]
        sig = jax.nn.sigmoid(gate)
        act = gate * sig
        hidden = act * up
        hidden_w.append((w * hidden).astype(BF16))
        route_part.append(jnp.sum(hidden * raw_grad[l], axis=1).reshape(groups, capacity))
        grad = w * raw_grad[l]
        preact_grad.append(
            jnp.concatenate(
                [grad * up * sig * (1.0 + gate * (1.0 - sig)), grad * act], axis=1
            ).astype(BF16)
        )
    layer_out = combine(
        [dot(hidden_w[l], down_weight[l], ((1,), (0,))).astype(BF16) for l in each], True
    )
    token_grad = combine(
        [dot(preact_grad[l], gate_up_weight[l], ((1,), (1,))).astype(BF16) for l in each], False
    )
    gate_up_grad = jnp.stack(
        [dot(x_slots[l], preact_grad[l], ((0,), (0,))).astype(BF16) for l in each]
    )
    down_grad = jnp.stack([dot(hidden_w[l], og_slots[l], ((0,), (0,))).astype(BF16) for l in each])
    route_token = jnp.stack(
        [jnp.sum(jnp.where(picks[l], route_part[l][:, :, None], 0.0), axis=1) for l in each]
    )
    route_all = jnp.sum(jnp.where(hits, route_token[..., None], 0.0), axis=0)
    route_all = reorder(route_all, where)
    route_grad = lax.psum_scatter(
        route_all.reshape(groups * tok_count, top_count),
        "expert",
        scatter_dimension=0,
        tiled=True,
    )
    return layer_out, token_grad, route_grad, gate_up_grad, down_grad


def solution(mesh):
    placed = (
        P("expert", "dp"),
        P("expert", None),
        P("expert", None),
        P("expert", "dp", None),
        P("expert", None, "dp"),
        P("expert", "dp"),
    )
    return jax.shard_map(
        local,
        mesh=mesh,
        in_specs=placed,
        out_specs=(
            P("expert", "dp"),
            P("expert", "dp"),
            P("expert", None),
            P("expert", "dp", None),
            P("expert", None, "dp"),
        ),
        check_vma=False,
    )
```

```python
import jax
import jax.numpy as jnp
from jax import lax
from jax.sharding import PartitionSpec as P

BF16 = jnp.bfloat16
F32 = jnp.float32


def dot(a, b, contract):
    return lax.dot_general(a, b, (contract, ((), ())), preferred_element_type=F32)


def dp_sum(part):
    size = lax.axis_size("dp")
    if size == 2:
        other = lax.ppermute(part, "dp", [(0, 1), (1, 0)])
        return part.astype(F32) + other.astype(F32)
    return lax.psum(part.astype(F32), "dp")


def ring_step(axis_size, step):
    chips = axis_size // 2
    order = [2 * i if 2 * i < chips else 2 * (chips - 1 - i) + 1 for i in range(chips)]
    return [
        (2 * order[i] + core, 2 * order[(i + step) % chips] + core)
        for i in range(chips)
        for core in range(2)
    ]


def move(array, step):
    return lax.ppermute(array, "expert", ring_step(lax.axis_size("expert"), step))


def swap(array):
    size = lax.axis_size("expert")
    return lax.ppermute(array, "expert", [(i, i ^ 1) for i in range(size)])


def hops(more):
    chips = lax.axis_size("expert") // 2
    return (chips // 2, chips - 1 - chips // 2) if more else (chips - 1 - chips // 2, chips // 2)


def after(array, earlier):
    return lax.optimization_barrier((array, earlier))[0]


def gather_ring(shard, more, behind=None):
    chips = lax.axis_size("expert") // 2
    ahead, back = hops(more)
    held = [None] * chips
    held[0] = shard
    first = shard if behind is None else after(shard, behind[0])
    second = shard if behind is None else after(shard, behind[1])
    for hop in range(1, max(ahead, back) + 1):
        if hop <= ahead:
            first = move(first, 1)
            held[hop] = first
        if hop <= back:
            second = move(second, -1)
            held[chips - hop] = second
    return jnp.stack(held + [swap(piece) for piece in held]), (first, second)


def scatter_ring(parts, more):
    chips = parts.shape[0] // 2
    ahead, back = hops(more)
    paired = swap(parts[chips:])

    def mine(o):
        return parts[o].astype(F32) + paired[o].astype(F32)

    first, second = mine(chips - ahead), mine(back)
    for hop in range(max(ahead, back) - 1, -1, -1):
        if hop < ahead:
            first = move(first.astype(BF16), 1).astype(F32)
            if hop:
                first = first + mine(chips - hop)
        if hop < back:
            second = move(second.astype(BF16), -1).astype(F32)
            if hop:
                second = second + mine(hop)
    return (mine(0) + first + second).astype(BF16)


def reorder(array, index):
    pick = index[:, None] == jnp.arange(array.shape[0])[None, :]
    return jnp.sum(jnp.where(pick[:, :, None, None], array[None], 0.0), axis=1)


def local(tokens, expert_ids, route_weights, gate_up_weight, down_weight, out_grad):
    tok_count, width = tokens.shape
    top_count = expert_ids.shape[1]
    groups = lax.axis_size("expert")
    local_count = gate_up_weight.shape[0]
    units = down_weight.shape[1]
    experts = local_count * groups
    capacity = 3 * tok_count * top_count // (2 * experts)
    rows = groups * capacity
    me = lax.axis_index("expert")

    chips = groups // 2
    spot = jnp.arange(groups)
    place = jnp.where(spot // 2 % 2 == 0, spot // 4, chips - 1 - spot // 4)
    my_place = jnp.where(me // 2 % 2 == 0, me // 4, chips - 1 - me // 4)
    where = (my_place - place) % chips + jnp.where(spot % 2 == me % 2, 0, chips)
    chip_at = (my_place - spot % chips) % chips
    chip_at = jnp.where(2 * chip_at < chips, 2 * chip_at, 2 * (chips - 1 - chip_at) + 1)
    order = 2 * chip_at + (me % 2 + spot // chips) % 2

    x_all, ends = gather_ring(tokens, True)
    og_all, _ = gather_ring(out_grad, False, ends)
    routing = lax.all_gather(
        jnp.concatenate([expert_ids.astype(F32), route_weights], axis=1),
        "expert",
        axis=0,
        tiled=True,
    ).reshape(groups, tok_count, 2 * top_count)
    routing = reorder(routing, order)

    ids = routing[..., :top_count]
    weights = routing[..., top_count:]
    mine = me * local_count + jnp.arange(local_count)
    hits = ids[None] == mine.astype(F32)[:, None, None, None]
    chosen = jnp.any(hits, axis=3)
    token_weight = jnp.sum(jnp.where(hits, weights[None], 0.0), axis=3)
    before = jnp.arange(tok_count)[:, None] < jnp.arange(tok_count)[None, :]
    rank = jnp.einsum(
        "lgt,tu->lgu", chosen.astype(BF16), before.astype(BF16), preferred_element_type=F32
    )
    places = jnp.arange(capacity, dtype=jnp.int32).astype(F32)
    picks = chosen[:, :, None, :] & (rank[:, :, None, :] == places[None, None, :, None])
    pick = picks.astype(BF16)
    slot_weight = jnp.sum(jnp.where(picks, token_weight[:, :, None, :], 0.0), axis=3)

    def slots(array, l):
        return (
            jnp.einsum("gct,gtd->gcd", pick[l], array, preferred_element_type=F32)
            .astype(BF16)
            .reshape(rows, width)
        )

    def total_of(values):
        total = sum(
            jnp.einsum(
                "gct,gcd->gtd",
                pick[l],
                values[l].reshape(groups, capacity, width),
                preferred_element_type=F32,
            )
            for l in range(local_count)
        )
        return total.astype(BF16)

    each = range(local_count)
    x_slots = [slots(x_all, l) for l in each]
    og_slots = [slots(og_all, l) for l in each]
    preact = [dp_sum(dot(x_slots[l], gate_up_weight[l], ((1,), (0,))).astype(BF16)) for l in each]
    hidden_w = []
    for l in each:
        gate, up = preact[l][:, :units], preact[l][:, units:]
        w = slot_weight[l].reshape(rows, 1)
        hidden_w.append((w * (gate * jax.nn.sigmoid(gate) * up)).astype(BF16))
    layer_total = total_of([dot(hidden_w[l], down_weight[l], ((1,), (0,))).astype(BF16) for l in each])
    grad_parts = [dot(og_slots[l], down_weight[l], ((1,), (1,))).astype(BF16) for l in each]
    grad_parts[-1], layer_total = lax.optimization_barrier((grad_parts[-1], layer_total))
    raw_grad = [dp_sum(part) for part in grad_parts]
    layer_out = scatter_ring(layer_total, True)
    preact_grad, route_part = [], []
    for l in each:
        w = slot_weight[l].reshape(rows, 1)
        gate, up = preact[l][:, :units], preact[l][:, units:]
        sig = jax.nn.sigmoid(gate)
        act = gate * sig
        hidden = act * up
        route_part.append(jnp.sum(hidden * raw_grad[l], axis=1).reshape(groups, capacity))
        grad = w * raw_grad[l]
        preact_grad.append(
            jnp.concatenate(
                [grad * up * sig * (1.0 + gate * (1.0 - sig)), grad * act], axis=1
            ).astype(BF16)
        )
    token_grad = scatter_ring(
        total_of([dot(preact_grad[l], gate_up_weight[l], ((1,), (1,))).astype(BF16) for l in each]),
        False,
    )
    gate_up_grad = jnp.stack(
        [dot(x_slots[l], preact_grad[l], ((0,), (0,))).astype(BF16) for l in each]
    )
    down_grad = jnp.stack([dot(hidden_w[l], og_slots[l], ((0,), (0,))).astype(BF16) for l in each])
    route_token = jnp.stack(
        [jnp.sum(jnp.where(picks[l], route_part[l][:, :, None], 0.0), axis=1) for l in each]
    )
    route_all = jnp.sum(jnp.where(hits, route_token[..., None], 0.0), axis=0)
    route_all = reorder(route_all, where)
    route_grad = lax.psum_scatter(
        route_all.reshape(groups * tok_count, top_count),
        "expert",
        scatter_dimension=0,
        tiled=True,
    )
    return layer_out, token_grad, route_grad, gate_up_grad, down_grad


def solution(mesh):
    placed = (
        P("expert", "dp"),
        P("expert", None),
        P("expert", None),
        P("expert", "dp", None),
        P("expert", None, "dp"),
        P("expert", "dp"),
    )
    return jax.shard_map(
        local,
        mesh=mesh,
        in_specs=placed,
        out_specs=(
            P("expert", "dp"),
            P("expert", "dp"),
            P("expert", None),
            P("expert", "dp", None),
            P("expert", None, "dp"),
        ),
        check_vma=False,
    )
```
